32 devices in a mesh: row: 4 (over z), col: 8 (over y, x, core).
Axes of the slice: x: 2, y: 2, z: 4, core: 2. Of those that a mesh axis runs over, the one named last changes fastest.
Arguments:
- coefficients: float32 [4, 8, 2, 128, 1024], P('row', 'col'), may hold values from -1 to 1
- greens: float32 [8, 4, 1024], P('col'), may hold values from -1 to 1
- cosine_weights: float32 [2, 2], replicated, may hold values from 0.3 to 1.2
- block_atoms: int32 [4, 8, 2, 2], P('row', 'col'), may hold values from 0 to 7
- pair_blocks: int32 [4, 8, 8, 2], P('row', 'col'), may hold values from 0 to 1
- owner_row: int32 [4, 8, 8, 1], P('row', 'col'), may hold values from 0 to 3; in each aligned block of 8 rows (0 to 7, 8 to 15, ..., all dimensions but the last counted through in order) at most 4 rows name the same one
- target_sub: int32 [4, 8, 8], P('row', 'col'), may hold values from 0 to 15
Outputs:
- response: float32 [2, 2048, 4096], P(None, 'row', 'col')
The draws below stay inside these ranges and needn't reach their ends.
Inputs may be any that keep to these rules, and one draw needn't show every extreme that they name: `owner_row`: among the 8 entries of one device (fixed first two indices) no row number occurs more than 4 times, and in every draw some device names one row exactly 4 times.
All inputs are finite; a program needn't handle non-finite values.
Results may differ from the reference program's by a relative error of at most 0.0029.
Values may be sent and summed in bfloat16 or wider, within the bound.
A program may use at most 64 MiB of HBM per device.

```python
import math
import jax
import jax.numpy as jnp
import numpy as np
from jax import lax

AUX_BLK = 128
BAS = 32
SUBS = 4
NBLK = 2
NCON = 8
TILE = 512
HALF = 4
CAP = 4
NATOM = 8
N_ROW = 4
N_COL = 8


def touch_ends(values, own_key, least, high):
    shape = values.shape
    place = [jax.random.randint(jax.random.fold_in(own_key, axis), (), 0, shape[axis]) for axis in range(len(shape))]
    values = values.at[tuple(place)].set(least)
    longest = shape.index(max(shape))
    place[longest] = (place[longest] + 1) % shape[longest]
    return values.at[tuple(place)].set(high)


def steps_of(stream_key, shape, cuts, low, top_value):
    def one(dim, shards_of):
        steps = jax.random.uniform(jax.random.fold_in(jax.random.fold_in(stream_key, 6), dim), (shards_of,), jnp.float32, low / len(cuts), top_value / len(cuts))
        return jnp.repeat(jnp.exp(steps), shape[dim] // shards_of).reshape((-1,) + (1,) * (len(shape) - dim - 1))

    gain = one(*cuts[0])
    for cut in cuts[1:]:
        gain = gain * one(*cut)
    return gain


def deal_out(key, own, number, rows, amount, top, most, skew):
    ranking = jax.random.permutation(key, amount)
    packed, common = shares(amount, rows * top, most, skew, True), shares(amount, rows * top, most, skew, False)
    places = jnp.arange(amount)

    def named(lengths, turn):
        used = int((lengths > 0).sum())
        fixed = max(1, used // 4)
        moved = fixed + (places - fixed + turn * (used - fixed)) % max(1, amount - fixed)
        return jnp.zeros((amount,), jnp.int32).at[ranking[jnp.where(places < fixed, places, moved)]].set(jnp.asarray(lengths, jnp.int32))

    lengths = jnp.where(number % 4 == 0, named(packed, number // 4), named(common, number - number // 4 - 1))
    mixed = jax.random.permutation(jax.random.fold_in(own, 3), amount)
    donor, receiver = mixed[0:amount // 2 * 2:2], mixed[1:amount // 2 * 2:2]
    margin = jnp.minimum(lengths[donor] - 1, most - lengths[receiver]) // 2
    margin = jnp.where((donor == ranking[0]) | (receiver == ranking[0]) | (lengths[receiver] == 0), 0, jnp.maximum(margin, 0))
    moved = jax.random.randint(jax.random.fold_in(own, 4), (amount // 2,), 0, 1 << 20) % (margin + 1)
    lengths = lengths.at[donor].add(-moved).at[receiver].add(moved)
    members = jnp.searchsorted(jnp.cumsum(lengths), jnp.arange(rows * top), side="right").astype(jnp.int32)
    table = members.reshape(top, rows).T
    table = table[jax.random.permutation(jax.random.fold_in(own, 1), rows)]
    turn = jax.random.randint(jax.random.fold_in(own, 2), (rows, 1), 0, top)
    return jnp.take_along_axis(table, (jnp.arange(top)[None, :] + turn) % top, axis=1)


def shares(count, total, most, skew, full):
    loads = [(1 << 20) // math.isqrt(standing ** skew) + 1 for standing in range(1, count + 1)]
    largest = most if full else min(most, max(-(-total // count), total * loads[0] // sum(loads)))
    least = 1 if total - largest >= count - 1 else 0
    holding, surplus = [largest] + [least] * (count - 1), total - largest - least * (count - 1)
    while surplus > 0:
        movable = [i for i in range(1, count) if holding[i] < largest] or [i for i in range(1, count) if holding[i] < most]
        mass, budget = sum([loads[i] for i in movable]), surplus
        for i in movable:
            extra = min(most - holding[i], max(1, budget * loads[i] // mass), surplus)
            holding[i] = holding[i] + extra
            surplus = surplus - extra
    return np.array(holding)


def centred(own_key, dims, width, reach, shards=(), kind=jnp.bfloat16):
    values = width * jax.random.normal(own_key, dims, jnp.float32)
    if shards:
        values = values * steps_of(own_key, dims, shards, -0.22, 0.18)
    return jnp.clip(values, -reach, reach).astype(kind)


def setup_inputs(seed: int = 0) -> dict:
    splits = jax.random.split(jax.random.key(seed), 8)
    coefficients = centred(splits[0], (N_ROW, N_COL, NBLK, AUX_BLK, BAS * BAS), 0.177, 1.0, ((0, 4), (1, 8)), jnp.float32)
    greens = centred(splits[1], (NATOM, 4, BAS * BAS), BAS ** -0.5, 1.0, ((0, 8),), jnp.float32)
    cosine_weights = jnp.clip(jax.random.uniform(splits[2], (2, 2), jnp.float32, 0.3, 1.2), 0.3, 1.2)
    block_atoms = touch_ends(jax.random.randint(splits[3], (N_ROW, N_COL, NBLK, 2), 0, NATOM), jax.random.fold_in(splits[3], 1), 0, NATOM - 1).astype(jnp.int32)
    pair_blocks = touch_ends(jax.random.randint(splits[4], (N_ROW, N_COL, NCON, 2), 0, NBLK), jax.random.fold_in(splits[4], 1), 0, NBLK - 1).astype(jnp.int32)
    owner_row_keys = jax.random.split(jax.random.fold_in(splits[5], 1), N_ROW * N_COL * NCON // NCON)
    owner_row_turns = jax.random.permutation(jax.random.fold_in(splits[5], 3), N_ROW * N_COL * NCON // NCON)
    owner_row = jax.vmap(lambda own, number: deal_out(jax.random.fold_in(splits[5], 2), own, number, NCON, N_ROW, 1, CAP, 2))(owner_row_keys, owner_row_turns).reshape((N_ROW, N_COL, NCON, 1))
    target_sub = touch_ends(jax.random.randint(splits[6], (N_ROW, N_COL, NCON), 0, SUBS * SUBS), jax.random.fold_in(splits[6], 1), 0, (SUBS * SUBS) - 1).astype(jnp.int32)
    return dict(coefficients=coefficients, greens=greens, cosine_weights=cosine_weights, block_atoms=block_atoms, pair_blocks=pair_blocks, owner_row=owner_row, target_sub=target_sub)


HIGH = lax.Precision.HIGHEST


def contract_device(blocks, table, weights, atom_pairs, block_pairs):
    count = blocks.shape[0]
    shaped = blocks.reshape(count, AUX_BLK, BAS, BAS)
    occupied = table[atom_pairs[:, 0]][:, 0:2].reshape(count, 2, BAS, BAS)
    virtual = table[atom_pairs[:, 1]][:, 2:4].reshape(count, 2, BAS, BAS)
    partway = jnp.einsum("bpmn,btns->btpms", shaped, virtual, precision=HIGH)
    contracted = jnp.einsum("btpms,btml->btpls", partway, occupied, precision=HIGH)
    combined = jnp.einsum("ft,btpls->bfpls", weights, contracted, precision=HIGH)
    combined = combined.reshape(count, 2, AUX_BLK, BAS * BAS)
    chosen_left = jnp.take(combined, block_pairs[:, 0], axis=0)
    chosen_right = jnp.take(blocks, block_pairs[:, 1], axis=0)
    product = jnp.einsum("kfap,kbp->kfab", chosen_left, chosen_right, precision=HIGH)
    return product.astype(jnp.bfloat16)


def reference(coefficients, greens, cosine_weights, block_atoms, pair_blocks, owner_row, target_sub):
    def column_tiles(column):
        blocks = lax.dynamic_index_in_dim(coefficients, column, 1, keepdims=False)
        atom_pairs = lax.dynamic_index_in_dim(block_atoms, column, 1, keepdims=False)
        block_pairs = lax.dynamic_index_in_dim(pair_blocks, column, 1, keepdims=False)
        owners = lax.dynamic_index_in_dim(owner_row, column, 1, keepdims=False)[:, :, 0]
        targets = lax.dynamic_index_in_dim(target_sub, column, 1, keepdims=False)
        pieces = jax.vmap(contract_device, in_axes=(0, None, None, 0, 0))(blocks, greens, cosine_weights, atom_pairs, block_pairs)
        row_ids = jnp.arange(N_ROW).astype(jnp.int32)
        sub_ids = jnp.arange(SUBS * SUBS).astype(jnp.int32)
        selector = ((owners[:, :, None, None] == row_ids[None, None, :, None]) & (targets[:, :, None, None] == sub_ids[None, None, None, :])).astype(jnp.float32)
        summed = jnp.einsum("rkos,rkfab->osfab", selector, pieces.astype(jnp.float32), precision=HIGH)
        summed = summed.reshape(N_ROW, SUBS, SUBS, 2, AUX_BLK, AUX_BLK)
        return summed.transpose(0, 3, 1, 4, 2, 5).reshape(N_ROW, 2, TILE, TILE)

    def mirrored_pair(index):
        first = column_tiles(index)
        second = column_tiles(index + HALF)
        return jnp.stack([first + jnp.swapaxes(second, -1, -2), second + jnp.swapaxes(first, -1, -2)])

    result = lax.map(mirrored_pair, jnp.arange(HALF).astype(jnp.int32))
    return result.transpose(3, 2, 4, 1, 0, 5).reshape(2, N_ROW * TILE, N_COL * TILE)
```

```python
import functools

import jax
import jax.numpy as jnp
from jax import lax
from jax.experimental import pallas as pl
from jax.experimental.pallas import tpu as pltpu
from jax.sharding import PartitionSpec as P

AUX_BLK = 128
BAS = 32
SUBS = 4
LABEL_ROWS = 16
BF = jnp.bfloat16
F32 = jnp.float32
MESH = pl.DeviceIdType.MESH


def split(x):
    high = x.astype(BF)
    return high, (x - high.astype(F32)).astype(BF)


def dot(a, b, dims=((1,), (0,))):
    return lax.dot_general(a, b, (dims, ((), ())), preferred_element_type=F32)


def dot3(a, b, dims=((1,), (0,))):
    return dot(a[0], b[0], dims) + (dot(a[0], b[1], dims) + dot(a[1], b[0], dims))


def onehot(shape, row_key, col_key):
    rows = lax.broadcasted_iota(jnp.int32, shape, 0)
    cols = lax.broadcasted_iota(jnp.int32, shape, 1)
    return row_key(rows) == col_key(cols)


def kernel(
    n_row, n_col, w_ref, atoms_ref, green_ref, label_ref, coef_ref, out_ref,
    table, gath, prods, send_g, recv_g, send_l, send_r, send_y, recv_z, recv_y,
):
    me_r = lax.axis_index("row")
    me_c = lax.axis_index("col")
    half = n_col // 2
    mirror = lax.rem(me_c + half, n_col)
    per = green_ref.shape[0]
    has_left = me_r > 0
    has_right = me_r < n_row - 1

    barrier = pltpu.get_barrier_semaphore()

    def greet(step, carry):
        peer = lax.rem(me_c + step, n_col)
        pl.semaphore_signal(barrier, inc=1, device_id=(me_r, peer), device_id_type=MESH)
        return carry

    lax.fori_loop(1, n_col, greet, 0)

    @pl.when(has_left)
    def _():
        pl.semaphore_signal(barrier, inc=1, device_id=(me_r - 1, me_c), device_id_type=MESH)

    @pl.when(has_right)
    def _():
        pl.semaphore_signal(barrier, inc=1, device_id=(me_r + 1, me_c), device_id_type=MESH)

    pl.semaphore_wait(
        barrier, n_col - 1 + has_left.astype(jnp.int32) + has_right.astype(jnp.int32)
    )

    def green_copy(slot, step, peer):
        return pltpu.make_async_remote_copy(
            src_ref=green_ref,
            dst_ref=table.at[slot],
            send_sem=send_g.at[step],
            recv_sem=recv_g.at[slot],
            device_id=(me_r, peer),
            device_id_type=MESH,
        )

    def send_green(step, carry):
        green_copy(me_c, step, lax.rem(me_c + step, n_col)).start()
        return carry

    lax.fori_loop(1, n_col, send_green, 0)

    def item(side, s, p):
        rows = 2 * AUX_BLK + (LABEL_ROWS if p == 0 else 0)
        return gath.at[side, s, p, pl.ds(0, rows)]

    def z_copy(s, p, to_right):
        sems = send_r if to_right else send_l
        return pltpu.make_async_remote_copy(
            src_ref=item(0, s, p),
            dst_ref=item(0, s, p),
            send_sem=sems.at[s, p],
            recv_sem=recv_z.at[s, p],
            device_id=(me_r + 1 if to_right else me_r - 1, me_c),
            device_id_type=MESH,
        )

    def y_copy(s, p):
        return pltpu.make_async_remote_copy(
            src_ref=item(0, s, p),
            dst_ref=item(1, s, p),
            send_sem=send_y.at[s, p],
            recv_sem=recv_y.at[s, p],
            device_id=(me_r, mirror),
            device_id_type=MESH,
        )

    out_ref[...] = jnp.zeros_like(out_ref)
    table[me_c] = green_ref[...]
    gath[0, me_r, 0, 2 * AUX_BLK :, :] = label_ref[...]
    coef = [split(coef_ref[q]) for q in range(2)]
    coef_all = tuple(jnp.concatenate([coef[q][h] for q in range(2)], 0) for h in range(2))
    wide = 8 * BAS
    rep_tile = onehot((wide, BAS), lambda i: i % BAS, lambda k: k).astype(BF)
    rep_each = onehot((wide, BAS), lambda i: i // 8, lambda k: k).astype(BF)
    lane_tile = jnp.concatenate(
        [onehot((4 * BAS, wide), lambda k: k, lambda j, t=t: (2 + t) * BAS + j % BAS) for t in range(2)], 1
    ).astype(F32).astype(BF)
    lane_each = jnp.concatenate(
        [onehot((4 * BAS, wide), lambda k: k, lambda j, t=t: t * BAS + j // 8) for t in range(2)], 1
    ).astype(F32).astype(BF)
    mask_tile = onehot((wide, 2 * wide), lambda i: i // BAS, lambda j: (j % wide) // BAS)
    mask_each = onehot((wide, 2 * wide), lambda i: i % 8, lambda j: j % 8)
    later = lax.broadcasted_iota(jnp.int32, (1, 2 * wide), 1) >= wide

    def wait_green(step, carry):
        peer = lax.rem(me_c + step, n_col)
        green_copy(peer, step, peer).wait_recv()
        return carry

    lax.fori_loop(1, n_col, wait_green, 0)

    for p in range(2):
        first = atoms_ref[p, 0]
        second = atoms_ref[p, 1]
        occ = split(table[first // per, first % per] if per > 1 else table[first, 0])
        vir = split(table[second // per, second % per] if per > 1 else table[second, 0])
        virt = []
        for part in vir:
            spread = dot(dot(rep_tile, part).astype(BF), lane_tile)
            spread = jnp.where(mask_tile, spread, 0.0)
            virt.append(jnp.concatenate([spread[:, :wide], spread[:, wide:]], 0).astype(BF))
        occupied = sum(dot(dot(rep_each, part).astype(BF), lane_each) for part in occ)
        occupied = jnp.where(mask_each, occupied, 0.0)
        left = split(
            jnp.concatenate(
                [occupied * jnp.where(later, w_ref[f, 1], w_ref[f, 0]) for f in range(2)], 0
            )
        )
        stacked = tuple(
            jnp.concatenate([part[:, m * wide : (m + 1) * wide] for m in range(4)], 0) for part in coef[p]
        )
        partway = dot3(virt, stacked, ((1,), (1,))).reshape(2, 8, 4, 8, 4 * AUX_BLK)
        lanes = []
        for s_hi in range(4):
            parts = [
                partway[:, :, s_hi, :, m * AUX_BLK : (m + 1) * AUX_BLK].reshape(2, 1, 8, 8, AUX_BLK)
                for m in range(4)
            ]
            lanes.append(jnp.concatenate(parts, 1).reshape(512, AUX_BLK))
        moved = split(jnp.concatenate(lanes, 1))
        combined = dot3(left, moved).reshape(2, BAS, 8, 4 * AUX_BLK)
        lanes = []
        for f in range(2):
            parts = [
                combined[f, :, :, s_hi * AUX_BLK : (s_hi + 1) * AUX_BLK].reshape(BAS, 1, 8, AUX_BLK)
                for s_hi in range(4)
            ]
            lanes.append(jnp.concatenate(parts, 1).reshape(BAS * BAS, AUX_BLK))
        right = split(jnp.concatenate(lanes, 1))
        gath[0, me_r, p, pl.ds(0, 2 * AUX_BLK), :] = dot3(coef_all, right).astype(BF)
        y_copy(me_r, p).start()

        @pl.when(has_right)
        def _(p=p):
            z_copy(me_r, p, True).start()

        @pl.when(has_left)
        def _(p=p):
            z_copy(me_r, p, False).start()

    def assemble(side, s):
        labels = gath[side, s, 0, 2 * AUX_BLK :, 0:AUX_BLK].astype(F32)
        code = jnp.where(labels[8:16] == me_r.astype(F32), labels[0:8], -1.0)
        for p in range(2):
            for q in range(2):
                for f in range(2):
                    block = gath[
                        side, s, p, q * AUX_BLK : (q + 1) * AUX_BLK, f * AUX_BLK : (f + 1) * AUX_BLK
                    ].astype(F32)
                    prods[f, 2 * p + q] = block.T if side == 0 else block

        def tile_row(i, carry):
            rows = pl.ds(pl.multiple_of(i * AUX_BLK, AUX_BLK), AUX_BLK)
            for j in range(SUBS):
                sub = i * SUBS + j if side == 0 else j * SUBS + i
                counts = [
                    jnp.sum(
                        jnp.where(code == (sub * 4 + k).astype(F32), 1.0, 0.0), axis=0, keepdims=True
                    )
                    for k in range(4)
                ]
                for f in range(2):
                    cols = slice(j * AUX_BLK, (j + 1) * AUX_BLK)
                    total = out_ref[f, rows, cols]
                    for k in range(4):
                        total += counts[k] * prods[f, k]
                    out_ref[f, rows, cols] = total
            return carry

        lax.fori_loop(0, SUBS, tile_row, 0)

    assemble(0, me_r)

    def pass_on(dist, carry):
        low = me_r - dist
        high = me_r + dist
        for p in range(2):

            @pl.when(low >= 0)
            def _(p=p):
                z_copy(low, p, True).wait_recv()
                y_copy(low, p).start()

                @pl.when(has_right)
                def _():
                    z_copy(low, p, True).start()

            @pl.when(high < n_row)
            def _(p=p):
                z_copy(high, p, False).wait_recv()
                y_copy(high, p).start()

                @pl.when(has_left)
                def _():
                    z_copy(high, p, False).start()

        @pl.when(low >= 0)
        def _():
            assemble(0, low)

        @pl.when(high < n_row)
        def _():
            assemble(0, high)

        return carry

    lax.fori_loop(1, n_row, pass_on, 0)

    def take_mirror(s):
        for p in range(2):
            y_copy(s, p).wait_recv()
        assemble(1, s)

    take_mirror(me_r)

    def mirrored(dist, carry):
        @pl.when(me_r - dist >= 0)
        def _():
            take_mirror(me_r - dist)

        @pl.when(me_r + dist < n_row)
        def _():
            take_mirror(me_r + dist)

        return carry

    lax.fori_loop(1, n_row, mirrored, 0)

    def drain_green(step, carry):
        green_copy(me_c, step, lax.rem(me_c + step, n_col)).wait_send()
        return carry

    lax.fori_loop(1, n_col, drain_green, 0)

    def drain(s, carry):
        for p in range(2):
            y_copy(s, p).wait_send()

            @pl.when(has_right & (s <= me_r))
            def _(p=p):
                z_copy(s, p, True).wait_send()

            @pl.when(has_left & (s >= me_r))
            def _(p=p):
                z_copy(s, p, False).wait_send()

        return carry

    lax.fori_loop(0, n_row, drain, 0)


def local(n_row, n_col, coefficients, greens, cosine_weights, block_atoms, pair_blocks, owner_row, target_sub):
    per = greens.shape[0]
    turned = greens.reshape(per, 4, BAS, BAS).transpose(0, 3, 1, 2).reshape(per, BAS, 4 * BAS)
    pairs = pair_blocks[0, 0]
    codes = target_sub[0, 0] * 4 + pairs[:, 0] * 2 + pairs[:, 1]
    labels = jnp.concatenate([codes, owner_row[0, 0, :, 0]]).astype(BF)
    labels = jnp.broadcast_to(labels[:, None], (LABEL_ROWS, 2 * AUX_BLK))
    vmem = pl.BlockSpec(memory_space=pltpu.VMEM)
    smem = pl.BlockSpec(memory_space=pltpu.SMEM)
    tile = SUBS * AUX_BLK
    dma = pltpu.SemaphoreType.DMA
    return pl.pallas_call(
        functools.partial(kernel, n_row, n_col),
        out_shape=jax.ShapeDtypeStruct((2, tile, tile), F32),
        in_specs=[smem, smem, vmem, vmem, vmem],
        out_specs=vmem,
        scratch_shapes=[
            pltpu.VMEM((n_col, per, BAS, 4 * BAS), F32),
            pltpu.VMEM((2, n_row, 2, 2 * AUX_BLK + LABEL_ROWS, 2 * AUX_BLK), BF),
            pltpu.VMEM((2, 4, AUX_BLK, AUX_BLK), F32),
            dma((n_col,)),
            dma((n_col,)),
            dma((n_row, 2)),
            dma((n_row, 2)),
            dma((n_row, 2)),
            dma((n_row, 2)),
            dma((n_row, 2)),
        ],
        compiler_params=pltpu.CompilerParams(
            collective_id=0, has_side_effects=True, vmem_limit_bytes=48 * 1024 * 1024
        ),
    )(cosine_weights, block_atoms[0, 0], turned, labels, coefficients[0, 0])


def solution(mesh):
    in_specs = (
        P("row", "col", None, None, None),
        P("col", None, None),
        P(),
        P("row", "col", None, None),
        P("row", "col", None, None),
        P("row", "col", None, None),
        P("row", "col", None),
    )
    return jax.shard_map(
        functools.partial(local, mesh.shape["row"], mesh.shape["col"]),
        mesh=mesh,
        in_specs=in_specs,
        out_specs=P(None, "row", "col"),
        check_vma=False,
    )
```

```python
import functools

import jax
import jax.numpy as jnp
from jax import lax
from jax.experimental import pallas as pl
from jax.experimental.pallas import tpu as pltpu
from jax.sharding import PartitionSpec as P

AUX_BLK = 128
BAS = 32
SUBS = 4
LABEL_ROWS = 16
BF = jnp.bfloat16
F32 = jnp.float32
MESH = pl.DeviceIdType.MESH


def split(x):
    high = x.astype(BF)
    return high, (x - high.astype(F32)).astype(BF)


def dot(a, b, dims=((1,), (0,))):
    return lax.dot_general(a, b, (dims, ((), ())), preferred_element_type=F32)


def dot3(a, b, dims=((1,), (0,))):
    return dot(a[0], b[0], dims) + (dot(a[0], b[1], dims) + dot(a[1], b[0], dims))


def onehot(shape, row_key, col_key):
    rows = lax.broadcasted_iota(jnp.int32, shape, 0)
    cols = lax.broadcasted_iota(jnp.int32, shape, 1)
    return row_key(rows) == col_key(cols)


def kernel(
    n_row, n_col, w_hbm, atoms_hbm, pairs_hbm, owners_hbm, targets_hbm, green_ref, coef_hbm, out_ref,
    w_ref, atoms_ref, pairs_ref, owners_ref, targets_ref, coef_ref,
    table, gath, prods, load, send_g, recv_g, send_l, send_r, send_y, recv_z, recv_y,
):
    me_r = lax.axis_index("row")
    me_c = lax.axis_index("col")
    half = n_col // 2
    mirror = lax.rem(me_c + half, n_col)
    per = green_ref.shape[0]
    has_left = me_r > 0
    has_right = me_r < n_row - 1

    sources = (coef_hbm, green_ref, w_hbm, atoms_hbm, pairs_hbm, owners_hbm, targets_hbm)
    places = (coef_ref, table.at[me_c], w_ref, atoms_ref, pairs_ref, owners_ref, targets_ref)
    loads = [
        pltpu.make_async_copy(source, place, load.at[number])
        for number, (source, place) in enumerate(zip(sources, places))
    ]
    for copy in loads:
        copy.start()
    barrier = pltpu.get_barrier_semaphore()

    def greet(step, carry):
        peer = lax.rem(me_c + step, n_col)
        pl.semaphore_signal(barrier, inc=1, device_id=(me_r, peer), device_id_type=MESH)
        return carry

    lax.fori_loop(1, n_col, greet, 0)

    @pl.when(has_left)
    def _():
        pl.semaphore_signal(barrier, inc=1, device_id=(me_r - 1, me_c), device_id_type=MESH)

    @pl.when(has_right)
    def _():
        pl.semaphore_signal(barrier, inc=1, device_id=(me_r + 1, me_c), device_id_type=MESH)

    pl.semaphore_wait(
        barrier, n_col - 1 + has_left.astype(jnp.int32) + has_right.astype(jnp.int32)
    )

    def green_copy(slot, step, peer):
        return pltpu.make_async_remote_copy(
            src_ref=green_ref,
            dst_ref=table.at[slot],
            send_sem=send_g.at[step],
            recv_sem=recv_g.at[slot],
            device_id=(me_r, peer),
            device_id_type=MESH,
        )

    def send_green(step, carry):
        green_copy(me_c, step, lax.rem(me_c + step, n_col)).start()
        return carry

    lax.fori_loop(1, n_col, send_green, 0)

    def item(side, s, p):
        rows = 2 * AUX_BLK + (LABEL_ROWS if p == 0 else 0)
        return gath.at[side, s, p, pl.ds(0, rows)]

    def z_copy(s, p, to_right):
        sems = send_r if to_right else send_l
        return pltpu.make_async_remote_copy(
            src_ref=item(0, s, p),
            dst_ref=item(0, s, p),
            send_sem=sems.at[s, p],
            recv_sem=recv_z.at[s, p],
            device_id=(me_r + 1 if to_right else me_r - 1, me_c),
            device_id_type=MESH,
        )

    def y_copy(s, p):
        return pltpu.make_async_remote_copy(
            src_ref=item(0, s, p),
            dst_ref=item(1, s, p),
            send_sem=send_y.at[s, p],
            recv_sem=recv_y.at[s, p],
            device_id=(me_r, mirror),
            device_id_type=MESH,
        )

    out_ref[...] = jnp.zeros_like(out_ref)
    wide = 8 * BAS
    flat = BAS * BAS
    low_tile = onehot((flat, wide), lambda k: k // BAS, lambda j: j % BAS).astype(F32).astype(BF)
    low_each = onehot((flat, wide), lambda k: k // BAS, lambda j: j // 8).astype(F32).astype(BF)
    rep_each = onehot((wide, BAS), lambda i: i // 8, lambda k: k).astype(F32).astype(BF)
    row_pick = onehot((BAS, flat), lambda i: i, lambda k: k % BAS)
    mask_tile = onehot((wide, wide), lambda i: i // BAS, lambda j: j // BAS)
    mask_each = onehot((wide, wide), lambda i: i % 8, lambda j: j % 8)
    for copy in loads:
        copy.wait()
    diagonal = onehot((8, 8), lambda i: i, lambda j: j)
    pairs = pairs_ref[...]
    codes = targets_ref[...] * 4 + pairs[0:1] * 2 + pairs[1:2]
    labels = [
        jnp.broadcast_to(
            jnp.sum(jnp.where(diagonal, row.astype(F32), 0.0), axis=1, keepdims=True), (8, 2 * AUX_BLK)
        )
        for row in (codes, owners_ref[...])
    ]
    gath[0, me_r, 0, 2 * AUX_BLK :, :] = jnp.concatenate(labels, 0).astype(BF)
    coef = [split(coef_ref[q]) for q in range(2)]
    coef_all = tuple(jnp.concatenate([coef[q][h] for q in range(2)], 0) for h in range(2))

    def wait_green(step, carry):
        peer = lax.rem(me_c + step, n_col)
        green_copy(peer, step, peer).wait_recv()
        return carry

    lax.fori_loop(1, n_col, wait_green, 0)

    for p in range(2):
        first = atoms_ref[p, 0]
        second = atoms_ref[p, 1]
        own = table[first // per, first % per] if per > 1 else table[first, 0]
        other = table[second // per, second % per] if per > 1 else table[second, 0]
        occ = split(
            jnp.concatenate([jnp.where(row_pick, own[t : t + 1], 0.0) for t in range(2)], 0)
        )
        vir = split(
            jnp.concatenate([jnp.where(row_pick, other[2 + t : 3 + t], 0.0) for t in range(2)], 0)
        )
        virt = []
        for part in vir:
            spread = dot(part, low_tile)
            blocks = [
                jnp.where(mask_tile, jnp.concatenate([spread[t * BAS : (t + 1) * BAS]] * 8, 0), 0.0)
                for t in range(2)
            ]
            virt.append(jnp.concatenate(blocks, 0).astype(BF))
        spread = [dot(part, low_each).astype(BF) for part in occ]
        occupied = [
            jnp.where(
                mask_each, sum(dot(rep_each, part[t * BAS : (t + 1) * BAS]) for part in spread), 0.0
            )
            for t in range(2)
        ]
        left = split(
            jnp.concatenate(
                [
                    jnp.concatenate([occupied[t] * w_ref[f, t] for t in range(2)], 1)
                    for f in range(2)
                ],
                0,
            )
        )
        stacked = tuple(
            jnp.concatenate([part[:, m * wide : (m + 1) * wide] for m in range(4)], 0) for part in coef[p]
        )
        partway = dot3(virt, stacked, ((1,), (1,))).reshape(2, 8, 4, 8, 4 * AUX_BLK)
        lanes = []
        for s_hi in range(4):
            parts = [
                partway[:, :, s_hi, :, m * AUX_BLK : (m + 1) * AUX_BLK].reshape(2, 1, 8, 8, AUX_BLK)
                for m in range(4)
            ]
            lanes.append(jnp.concatenate(parts, 1).reshape(512, AUX_BLK))
        moved = split(jnp.concatenate(lanes, 1))
        combined = dot3(left, moved).reshape(2, BAS, 8, 4 * AUX_BLK)
        lanes = []
        for f in range(2):
            parts = [
                combined[f, :, :, s_hi * AUX_BLK : (s_hi + 1) * AUX_BLK].reshape(BAS, 1, 8, AUX_BLK)
                for s_hi in range(4)
            ]
            lanes.append(jnp.concatenate(parts, 1).reshape(BAS * BAS, AUX_BLK))
        right = split(jnp.concatenate(lanes, 1))
        gath[0, me_r, p, pl.ds(0, 2 * AUX_BLK), :] = dot3(coef_all, right).astype(BF)
        y_copy(me_r, p).start()

        @pl.when(has_right)
        def _(p=p):
            z_copy(me_r, p, True).start()

        @pl.when(has_left)
        def _(p=p):
            z_copy(me_r, p, False).start()

    def assemble(side, s):
        labels = gath[side, s, 0, 2 * AUX_BLK :, 0:AUX_BLK].astype(F32)
        code = jnp.where(labels[8:16] == me_r.astype(F32), labels[0:8], -1.0)
        for p in range(2):
            for q in range(2):
                for f in range(2):
                    block = gath[
                        side, s, p, q * AUX_BLK : (q + 1) * AUX_BLK, f * AUX_BLK : (f + 1) * AUX_BLK
                    ].astype(F32)
                    prods[f, 2 * p + q] = block.T if side == 0 else block

        def tile_row(i, carry):
            rows = pl.ds(pl.multiple_of(i * AUX_BLK, AUX_BLK), AUX_BLK)
            for j in range(SUBS):
                sub = i * SUBS + j if side == 0 else j * SUBS + i
                counts = [
                    jnp.sum(
                        jnp.where(code == (sub * 4 + k).astype(F32), 1.0, 0.0), axis=0, keepdims=True
                    )
                    for k in range(4)
                ]
                for f in range(2):
                    cols = slice(j * AUX_BLK, (j + 1) * AUX_BLK)
                    total = out_ref[f, rows, cols]
                    for k in range(4):
                        total += counts[k] * prods[f, k]
                    out_ref[f, rows, cols] = total
            return carry

        lax.fori_loop(0, SUBS, tile_row, 0)

    assemble(0, me_r)

    def pass_on(dist, carry):
        low = me_r - dist
        high = me_r + dist
        for p in range(2):

            @pl.when(low >= 0)
            def _(p=p):
                z_copy(low, p, True).wait_recv()
                y_copy(low, p).start()

                @pl.when(has_right)
                def _():
                    z_copy(low, p, True).start()

            @pl.when(high < n_row)
            def _(p=p):
                z_copy(high, p, False).wait_recv()
                y_copy(high, p).start()

                @pl.when(has_left)
                def _():
                    z_copy(high, p, False).start()

        @pl.when(low >= 0)
        def _():
            assemble(0, low)

        @pl.when(high < n_row)
        def _():
            assemble(0, high)

        return carry

    lax.fori_loop(1, n_row, pass_on, 0)

    def take_mirror(s):
        for p in range(2):
            y_copy(s, p).wait_recv()
        assemble(1, s)

    take_mirror(me_r)

    def mirrored(dist, carry):
        @pl.when(me_r - dist >= 0)
        def _():
            take_mirror(me_r - dist)

        @pl.when(me_r + dist < n_row)
        def _():
            take_mirror(me_r + dist)

        return carry

    lax.fori_loop(1, n_row, mirrored, 0)

    def drain_green(step, carry):
        green_copy(me_c, step, lax.rem(me_c + step, n_col)).wait_send()
        return carry

    lax.fori_loop(1, n_col, drain_green, 0)

    def drain(s, carry):
        for p in range(2):
            y_copy(s, p).wait_send()

            @pl.when(has_right & (s <= me_r))
            def _(p=p):
                z_copy(s, p, True).wait_send()

            @pl.when(has_left & (s >= me_r))
            def _(p=p):
                z_copy(s, p, False).wait_send()

        return carry

    lax.fori_loop(0, n_row, drain, 0)


def local(n_row, n_col, coefficients, greens, cosine_weights, block_atoms, pair_blocks, owner_row, target_sub):
    per = greens.shape[0]
    hbm = pl.BlockSpec(memory_space=pltpu.HBM)
    vmem = pl.BlockSpec(memory_space=pltpu.VMEM)
    tile = SUBS * AUX_BLK
    dma = pltpu.SemaphoreType.DMA
    return pl.pallas_call(
        functools.partial(kernel, n_row, n_col),
        out_shape=jax.ShapeDtypeStruct((2, tile, tile), F32),
        in_specs=[hbm] * 7,
        out_specs=vmem,
        scratch_shapes=[
            pltpu.SMEM((2, 2), F32),
            pltpu.SMEM((2, 2), jnp.int32),
            pltpu.VMEM((2, 8), jnp.int32),
            pltpu.VMEM((1, 8), jnp.int32),
            pltpu.VMEM((1, 8), jnp.int32),
            pltpu.VMEM((2, AUX_BLK, BAS * BAS), F32),
            pltpu.VMEM((n_col, per, 4, BAS * BAS), F32),
            pltpu.VMEM((2, n_row, 2, 2 * AUX_BLK + LABEL_ROWS, 2 * AUX_BLK), BF),
            pltpu.VMEM((2, 4, AUX_BLK, AUX_BLK), F32),
            dma((7,)),
            dma((n_col,)),
            dma((n_col,)),
            dma((n_row, 2)),
            dma((n_row, 2)),
            dma((n_row, 2)),
            dma((n_row, 2)),
            dma((n_row, 2)),
        ],
        compiler_params=pltpu.CompilerParams(
            collective_id=0, has_side_effects=True, vmem_limit_bytes=60 * 1024 * 1024
        ),
    )(
        cosine_weights,
        block_atoms[0, 0],
        pair_blocks[0, 0].T,
        owner_row[0, 0].T,
        target_sub[0],
        greens,
        coefficients[0, 0],
    )


def solution(mesh):
    in_specs = (
        P("row", "col", None, None, None),
        P("col", None, None),
        P(),
        P("row", "col", None, None),
        P("row", "col", None, None),
        P("row", "col", None, None),
        P("row", "col", None),
    )
    return jax.shard_map(
        functools.partial(local, mesh.shape["row"], mesh.shape["col"]),
        mesh=mesh,
        in_specs=in_specs,
        out_specs=P(None, "row", "col"),
        check_vma=False,
    )
```

```python
import functools

import jax
import jax.numpy as jnp
from jax import lax
from jax.experimental import pallas as pl
from jax.experimental.pallas import tpu as pltpu
from jax.sharding import PartitionSpec as P

AUX_BLK = 128
BAS = 32
SUBS = 4
LABEL_ROWS = 16
BF = jnp.bfloat16
F32 = jnp.float32
MESH = pl.DeviceIdType.MESH


def split(x):
    high = x.astype(BF)
    return high, (x - high.astype(F32)).astype(BF)


def dot(a, b, dims=((1,), (0,))):
    return lax.dot_general(a, b, (dims, ((), ())), preferred_element_type=F32)


def dot3(a, b, dims=((1,), (0,))):
    return dot(a[0], b[0], dims) + (dot(a[0], b[1], dims) + dot(a[1], b[0], dims))


def onehot(shape, row_key, col_key):
    rows = lax.broadcasted_iota(jnp.int32, shape, 0)
    cols = lax.broadcasted_iota(jnp.int32, shape, 1)
    return row_key(rows) == col_key(cols)


def kernel(
    n_row, n_col, w_hbm, atoms_hbm, pairs_hbm, owners_hbm, targets_hbm, green_ref, coef_hbm, out_ref,
    w_ref, atoms_ref, pairs_ref, owners_ref, targets_ref, coef_ref,
    table, gath, prods, load, send_g, recv_g, send_l, send_r, send_y, send_m, recv_z, recv_y,
):
    me_r = lax.axis_index("row")
    me_c = lax.axis_index("col")
    half = n_col // 2
    mirror = lax.rem(me_c + half, n_col)
    per = green_ref.shape[0]
    buddy = me_r + 1 - 2 * lax.rem(me_r, 2)
    has_left = me_r > 0
    has_right = me_r < n_row - 1

    sources = (coef_hbm, green_ref, w_hbm, atoms_hbm, pairs_hbm, owners_hbm, targets_hbm)
    places = (coef_ref, table.at[me_c], w_ref, atoms_ref, pairs_ref, owners_ref, targets_ref)
    loads = [
        pltpu.make_async_copy(source, place, load.at[number])
        for number, (source, place) in enumerate(zip(sources, places))
    ]
    for copy in loads:
        copy.start()
    barrier = pltpu.get_barrier_semaphore()

    def greet(step, carry):
        peer = lax.rem(me_c + step, n_col)
        pl.semaphore_signal(barrier, inc=1, device_id=(me_r, peer), device_id_type=MESH)
        return carry

    lax.fori_loop(1, n_col, greet, 0)

    @pl.when(has_left)
    def _():
        pl.semaphore_signal(barrier, inc=1, device_id=(me_r - 1, me_c), device_id_type=MESH)

    @pl.when(has_right)
    def _():
        pl.semaphore_signal(barrier, inc=1, device_id=(me_r + 1, me_c), device_id_type=MESH)

    out_ref[...] = jnp.zeros_like(out_ref)
    pl.semaphore_wait(
        barrier, n_col - 1 + has_left.astype(jnp.int32) + has_right.astype(jnp.int32)
    )

    def green_copy(slot, step, peer):
        return pltpu.make_async_remote_copy(
            src_ref=green_ref,
            dst_ref=table.at[slot],
            send_sem=send_g.at[step],
            recv_sem=recv_g.at[slot],
            device_id=(me_r, peer),
            device_id_type=MESH,
        )

    def send_green(step, carry):
        green_copy(me_c, step, lax.rem(me_c + step, n_col)).start()
        return carry

    lax.fori_loop(1, n_col, send_green, 0)

    def item(side, s, p):
        rows = 2 * AUX_BLK + (LABEL_ROWS if p == 0 else 0)
        return gath.at[side, s, p, pl.ds(0, rows)]

    def z_copy(s, p, to_right):
        sems = send_r if to_right else send_l
        return pltpu.make_async_remote_copy(
            src_ref=item(0, s, p),
            dst_ref=item(0, s, p),
            send_sem=sems.at[s, p],
            recv_sem=recv_z.at[s, p],
            device_id=(me_r + 1 if to_right else me_r - 1, me_c),
            device_id_type=MESH,
        )

    def y_copy(s, p):
        return pltpu.make_async_remote_copy(
            src_ref=item(0, s, p),
            dst_ref=item(1, s, p),
            send_sem=send_y.at[s, p],
            recv_sem=recv_y.at[s, p],
            device_id=(me_r, mirror),
            device_id_type=MESH,
        )

    wide = 8 * BAS
    flat = BAS * BAS
    low_tile = onehot((flat, wide), lambda k: k // BAS, lambda j: j % BAS).astype(F32).astype(BF)
    low_each = onehot((flat, wide), lambda k: k // BAS, lambda j: j // 8).astype(F32).astype(BF)
    rep_each = onehot((wide, BAS), lambda i: i // 8, lambda k: k).astype(F32).astype(BF)
    row_pick = onehot((BAS, flat), lambda i: i, lambda k: k % BAS)
    mask_tile = onehot((wide, wide), lambda i: i // BAS, lambda j: j // BAS)
    mask_each = onehot((wide, wide), lambda i: i % 8, lambda j: j % 8)
    for copy in loads:
        copy.wait()
    diagonal = onehot((8, 8), lambda i: i, lambda j: j)
    pairs = pairs_ref[...]
    codes = targets_ref[...] * 4 + pairs[0:1] * 2 + pairs[1:2]
    labels = [
        jnp.broadcast_to(
            jnp.sum(jnp.where(diagonal, row.astype(F32), 0.0), axis=1, keepdims=True), (8, 2 * AUX_BLK)
        )
        for row in (codes, owners_ref[...])
    ]
    gath[0, me_r, 0, 2 * AUX_BLK :, :] = jnp.concatenate(labels, 0).astype(BF)
    coef = [split(coef_ref[q]) for q in range(2)]
    coef_all = tuple(jnp.concatenate([coef[q][h] for q in range(2)], 0) for h in range(2))

    def wait_green(step, carry):
        peer = lax.rem(me_c + step, n_col)
        green_copy(peer, step, peer).wait_recv()
        return carry

    lax.fori_loop(1, n_col, wait_green, 0)

    for p in range(2):
        first = atoms_ref[p, 0]
        second = atoms_ref[p, 1]
        own = table[first // per, first % per] if per > 1 else table[first, 0]
        other = table[second // per, second % per] if per > 1 else table[second, 0]
        occ = split(
            jnp.concatenate([jnp.where(row_pick, own[t : t + 1], 0.0) for t in range(2)], 0)
        )
        vir = split(
            jnp.concatenate([jnp.where(row_pick, other[2 + t : 3 + t], 0.0) for t in range(2)], 0)
        )
        virt = []
        for part in vir:
            spread = dot(part, low_tile)
            blocks = [
                jnp.where(mask_tile, jnp.concatenate([spread[t * BAS : (t + 1) * BAS]] * 8, 0), 0.0)
                for t in range(2)
            ]
            virt.append(jnp.concatenate(blocks, 0).astype(BF))
        spread = [dot(part, low_each).astype(BF) for part in occ]
        occupied = [
            jnp.where(
                mask_each, sum(dot(rep_each, part[t * BAS : (t + 1) * BAS]) for part in spread), 0.0
            )
            for t in range(2)
        ]
        left = split(
            jnp.concatenate(
                [
                    jnp.concatenate([occupied[t] * w_ref[f, t] for t in range(2)], 1)
                    for f in range(2)
                ],
                0,
            )
        )
        stacked = tuple(
            jnp.concatenate([part[:, m * wide : (m + 1) * wide] for m in range(4)], 0) for part in coef[p]
        )
        partway = dot3(virt, stacked, ((1,), (1,))).reshape(2, 8, 4, 8, 4 * AUX_BLK)
        lanes = []
        for s_hi in range(4):
            parts = [
                partway[:, :, s_hi, :, m * AUX_BLK : (m + 1) * AUX_BLK].reshape(2, 1, 8, 8, AUX_BLK)
                for m in range(4)
            ]
            lanes.append(jnp.concatenate(parts, 1).reshape(512, AUX_BLK))
        moved = split(jnp.concatenate(lanes, 1))
        combined = dot3(left, moved).reshape(2, BAS, 8, 4 * AUX_BLK)
        lanes = []
        for f in range(2):
            parts = [
                combined[f, :, :, s_hi * AUX_BLK : (s_hi + 1) * AUX_BLK].reshape(BAS, 1, 8, AUX_BLK)
                for s_hi in range(4)
            ]
            lanes.append(jnp.concatenate(parts, 1).reshape(BAS * BAS, AUX_BLK))
        right = split(jnp.concatenate(lanes, 1))
        gath[0, me_r, p, pl.ds(0, 2 * AUX_BLK), :] = dot3(coef_all, right).astype(BF)
        y_copy(me_r, p).start()

        @pl.when(has_right)
        def _(p=p):
            z_copy(me_r, p, True).start()

        @pl.when(has_left)
        def _(p=p):
            z_copy(me_r, p, False).start()

    def assemble(side, s):
        labels = gath[side, s, 0, 2 * AUX_BLK :, 0:AUX_BLK].astype(F32)
        code = jnp.where(labels[8:16] == me_r.astype(F32), labels[0:8], -1.0)
        for p in range(2):
            for q in range(2):
                for f in range(2):
                    block = gath[
                        side, s, p, q * AUX_BLK : (q + 1) * AUX_BLK, f * AUX_BLK : (f + 1) * AUX_BLK
                    ].astype(F32)
                    prods[f, 2 * p + q] = block.T if side == 0 else block

        def tile_row(i, carry):
            rows = pl.ds(pl.multiple_of(i * AUX_BLK, AUX_BLK), AUX_BLK)
            for j in range(SUBS):
                sub = i * SUBS + j if side == 0 else j * SUBS + i
                counts = [
                    jnp.sum(
                        jnp.where(code == (sub * 4 + k).astype(F32), 1.0, 0.0), axis=0, keepdims=True
                    )
                    for k in range(4)
                ]
                for f in range(2):
                    cols = slice(j * AUX_BLK, (j + 1) * AUX_BLK)
                    total = out_ref[f, rows, cols]
                    for k in range(4):
                        total += counts[k] * prods[f, k]
                    out_ref[f, rows, cols] = total
            return carry

        lax.fori_loop(0, SUBS, tile_row, 0)

    assemble(0, me_r)

    def handed_copy():
        return pltpu.make_async_remote_copy(
            src_ref=item(1, me_r, 1),
            dst_ref=item(1, me_r, 1),
            send_sem=send_m.at[0],
            recv_sem=recv_y.at[me_r, 1],
            device_id=(buddy, me_c),
            device_id_type=MESH,
        )

    def pass_mirror(s, p):
        if p == 0:
            y_copy(s, p).start()
        else:

            @pl.when(s != buddy)
            def _():
                y_copy(s, p).start()

    def pass_on(dist, carry):
        low = me_r - dist
        high = me_r + dist
        for p in range(2):

            @pl.when(low >= 0)
            def _(p=p):
                z_copy(low, p, True).wait_recv()
                pass_mirror(low, p)

                @pl.when(has_right)
                def _():
                    z_copy(low, p, True).start()

            @pl.when(high < n_row)
            def _(p=p):
                z_copy(high, p, False).wait_recv()
                pass_mirror(high, p)

                @pl.when(has_left)
                def _():
                    z_copy(high, p, False).start()

        @pl.when(low >= 0)
        def _():
            assemble(0, low)

        @pl.when(high < n_row)
        def _():
            assemble(0, high)

        return carry

    lax.fori_loop(1, n_row, pass_on, 0)

    y_copy(me_r, 1).wait_recv()
    handed_copy().start()
    y_copy(me_r, 0).wait_recv()
    assemble(1, me_r)

    def take_mirror(s):
        for p in range(2):
            y_copy(s, p).wait_recv()
        assemble(1, s)

    def mirrored(dist, carry):
        low = me_r - dist
        high = me_r + dist

        @pl.when((low >= 0) & (low != buddy))
        def _():
            take_mirror(low)

        @pl.when((high < n_row) & (high != buddy))
        def _():
            take_mirror(high)

        return carry

    lax.fori_loop(1, n_row, mirrored, 0)
    take_mirror(buddy)
    handed_copy().wait_send()

    def drain_green(step, carry):
        green_copy(me_c, step, lax.rem(me_c + step, n_col)).wait_send()
        return carry

    lax.fori_loop(1, n_col, drain_green, 0)

    def drain(s, carry):
        for p in range(2):

            @pl.when((s != buddy) if p == 1 else (s >= 0))
            def _(p=p):
                y_copy(s, p).wait_send()

            @pl.when(has_right & (s <= me_r))
            def _(p=p):
                z_copy(s, p, True).wait_send()

            @pl.when(has_left & (s >= me_r))
            def _(p=p):
                z_copy(s, p, False).wait_send()

        return carry

    lax.fori_loop(0, n_row, drain, 0)


def local(n_row, n_col, coefficients, greens, cosine_weights, block_atoms, pair_blocks, owner_row, target_sub):
    per = greens.shape[0]
    hbm = pl.BlockSpec(memory_space=pltpu.HBM)
    vmem = pl.BlockSpec(memory_space=pltpu.VMEM)
    tile = SUBS * AUX_BLK
    dma = pltpu.SemaphoreType.DMA
    return pl.pallas_call(
        functools.partial(kernel, n_row, n_col),
        out_shape=pltpu.VMEM((2, tile, tile), F32),
        in_specs=[hbm] * 7,
        out_specs=vmem,
        scratch_shapes=[
            pltpu.SMEM((2, 2), F32),
            pltpu.SMEM((2, 2), jnp.int32),
            pltpu.VMEM((2, 8), jnp.int32),
            pltpu.VMEM((1, 8), jnp.int32),
            pltpu.VMEM((1, 8), jnp.int32),
            pltpu.VMEM((2, AUX_BLK, BAS * BAS), F32),
            pltpu.VMEM((n_col, per, 4, BAS * BAS), F32),
            pltpu.VMEM((2, n_row, 2, 2 * AUX_BLK + LABEL_ROWS, 2 * AUX_BLK), BF),
            pltpu.VMEM((2, 4, AUX_BLK, AUX_BLK), F32),
            dma((7,)),
            dma((n_col,)),
            dma((n_col,)),
            dma((n_row, 2)),
            dma((n_row, 2)),
            dma((n_row, 2)),
            dma((1,)),
            dma((n_row, 2)),
            dma((n_row, 2)),
        ],
        compiler_params=pltpu.CompilerParams(
            collective_id=0, has_side_effects=True, vmem_limit_bytes=60 * 1024 * 1024
        ),
    )(
        cosine_weights,
        block_atoms[0, 0],
        pair_blocks[0, 0].T,
        owner_row[0, 0].T,
        target_sub[0],
        greens,
        coefficients[0, 0],
    )


def solution(mesh):
    in_specs = (
        P("row", "col", None, None, None),
        P("col", None, None),
        P(),
        P("row", "col", None, None),
        P("row", "col", None, None),
        P("row", "col", None, None),
        P("row", "col", None),
    )
    return jax.shard_map(
        functools.partial(local, mesh.shape["row"], mesh.shape["col"]),
        mesh=mesh,
        in_specs=in_specs,
        out_specs=P(None, "row", "col"),
        check_vma=False,
    )
```

```python
import functools

import jax
import jax.numpy as jnp
from jax import lax
from jax.experimental import pallas as pl
from jax.experimental.pallas import tpu as pltpu
from jax.sharding import PartitionSpec as P

AUX_BLK = 128
BAS = 32
SUBS = 4
LABEL_ROWS = 16
BF = jnp.bfloat16
F32 = jnp.float32
MESH = pl.DeviceIdType.MESH


def split(x):
    high = x.astype(BF)
    return high, (x - high.astype(F32)).astype(BF)


def dot(a, b, dims=((1,), (0,))):
    return lax.dot_general(a, b, (dims, ((), ())), preferred_element_type=F32)


def dot3(a, b, dims=((1,), (0,))):
    return dot(a[0], b[0], dims) + (dot(a[0], b[1], dims) + dot(a[1], b[0], dims))


def onehot(shape, row_key, col_key):
    rows = lax.broadcasted_iota(jnp.int32, shape, 0)
    cols = lax.broadcasted_iota(jnp.int32, shape, 1)
    return row_key(rows) == col_key(cols)


def kernel(
    n_row, n_col, w_hbm, atoms_hbm, pairs_hbm, owners_hbm, targets_hbm, green_ref, coef_hbm, out_ref,
    w_ref, atoms_ref, pairs_ref, owners_ref, targets_ref, coef_ref,
    table, gath, prods, load, send_g, recv_g, send_z, send_y, send_m, recv_z, recv_y,
):
    me_r = lax.axis_index("row")
    me_c = lax.axis_index("col")
    half = n_col // 2
    mirror = lax.rem(me_c + half, n_col)
    per = green_ref.shape[0]
    buddy = me_r + 1 - 2 * lax.rem(me_r, 2)

    sources = (coef_hbm, green_ref, w_hbm, atoms_hbm, pairs_hbm, owners_hbm, targets_hbm)
    places = (coef_ref, table.at[me_c], w_ref, atoms_ref, pairs_ref, owners_ref, targets_ref)
    loads = [
        pltpu.make_async_copy(source, place, load.at[number])
        for number, (source, place) in enumerate(zip(sources, places))
    ]
    for copy in loads:
        copy.start()
    barrier = pltpu.get_barrier_semaphore()

    def greet(step, carry):
        peer = lax.rem(me_c + step, n_col)
        pl.semaphore_signal(barrier, inc=1, device_id=(me_r, peer), device_id_type=MESH)
        return carry

    lax.fori_loop(1, n_col, greet, 0)

    def greet_row(step, carry):
        peer = lax.rem(me_r + step, n_row)
        pl.semaphore_signal(barrier, inc=1, device_id=(peer, me_c), device_id_type=MESH)
        return carry

    lax.fori_loop(1, n_row, greet_row, 0)
    out_ref[...] = jnp.zeros_like(out_ref)
    pl.semaphore_wait(barrier, n_col + n_row - 2)

    def green_copy(slot, step, peer):
        return pltpu.make_async_remote_copy(
            src_ref=green_ref,
            dst_ref=table.at[slot],
            send_sem=send_g.at[step],
            recv_sem=recv_g.at[slot],
            device_id=(me_r, peer),
            device_id_type=MESH,
        )

    def send_green(step, carry):
        green_copy(me_c, step, lax.rem(me_c + step, n_col)).start()
        return carry

    lax.fori_loop(1, n_col, send_green, 0)

    def item(side, s, p):
        rows = 2 * AUX_BLK + (LABEL_ROWS if p == 0 else 0)
        return gath.at[side, s, p, pl.ds(0, rows)]

    def z_copy(s, p, peer):
        return pltpu.make_async_remote_copy(
            src_ref=item(0, s, p),
            dst_ref=item(0, s, p),
            send_sem=send_z.at[peer, p],
            recv_sem=recv_z.at[s, p],
            device_id=(peer, me_c),
            device_id_type=MESH,
        )

    def y_copy(s, p):
        return pltpu.make_async_remote_copy(
            src_ref=item(0, s, p),
            dst_ref=item(1, s, p),
            send_sem=send_y.at[s, p],
            recv_sem=recv_y.at[s, p],
            device_id=(me_r, mirror),
            device_id_type=MESH,
        )

    wide = 8 * BAS
    flat = BAS * BAS
    low_tile = onehot((flat, wide), lambda k: k // BAS, lambda j: j % BAS).astype(F32).astype(BF)
    low_each = onehot((flat, wide), lambda k: k // BAS, lambda j: j // 8).astype(F32).astype(BF)
    rep_each = onehot((wide, BAS), lambda i: i // 8, lambda k: k).astype(F32).astype(BF)
    row_pick = onehot((BAS, flat), lambda i: i, lambda k: k % BAS)
    mask_tile = onehot((wide, wide), lambda i: i // BAS, lambda j: j // BAS)
    mask_each = onehot((wide, wide), lambda i: i % 8, lambda j: j % 8)
    for copy in loads:
        copy.wait()
    diagonal = onehot((8, 8), lambda i: i, lambda j: j)
    pairs = pairs_ref[...]
    codes = targets_ref[...] * 4 + pairs[0:1] * 2 + pairs[1:2]
    labels = [
        jnp.broadcast_to(
            jnp.sum(jnp.where(diagonal, row.astype(F32), 0.0), axis=1, keepdims=True), (8, 2 * AUX_BLK)
        )
        for row in (codes, owners_ref[...])
    ]
    gath[0, me_r, 0, 2 * AUX_BLK :, :] = jnp.concatenate(labels, 0).astype(BF)
    coef = [split(coef_ref[q]) for q in range(2)]
    coef_all = tuple(jnp.concatenate([coef[q][h] for q in range(2)], 0) for h in range(2))

    def wait_green(step, carry):
        peer = lax.rem(me_c + step, n_col)
        green_copy(peer, step, peer).wait_recv()
        return carry

    lax.fori_loop(1, n_col, wait_green, 0)

    for p in range(2):
        first = atoms_ref[p, 0]
        second = atoms_ref[p, 1]
        own = table[first // per, first % per] if per > 1 else table[first, 0]
        other = table[second // per, second % per] if per > 1 else table[second, 0]
        occ = split(
            jnp.concatenate([jnp.where(row_pick, own[t : t + 1], 0.0) for t in range(2)], 0)
        )
        vir = split(
            jnp.concatenate([jnp.where(row_pick, other[2 + t : 3 + t], 0.0) for t in range(2)], 0)
        )
        virt = []
        for part in vir:
            spread = dot(part, low_tile)
            blocks = [
                jnp.where(mask_tile, jnp.concatenate([spread[t * BAS : (t + 1) * BAS]] * 8, 0), 0.0)
                for t in range(2)
            ]
            virt.append(jnp.concatenate(blocks, 0).astype(BF))
        spread = [dot(part, low_each).astype(BF) for part in occ]
        occupied = [
            jnp.where(
                mask_each, sum(dot(rep_each, part[t * BAS : (t + 1) * BAS]) for part in spread), 0.0
            )
            for t in range(2)
        ]
        left = split(
            jnp.concatenate(
                [
                    jnp.concatenate([occupied[t] * w_ref[f, t] for t in range(2)], 1)
                    for f in range(2)
                ],
                0,
            )
        )
        stacked = tuple(
            jnp.concatenate([part[:, m * wide : (m + 1) * wide] for m in range(4)], 0) for part in coef[p]
        )
        partway = dot3(virt, stacked, ((1,), (1,))).reshape(2, 8, 4, 8, 4 * AUX_BLK)
        lanes = []
        for s_hi in range(4):
            parts = [
                partway[:, :, s_hi, :, m * AUX_BLK : (m + 1) * AUX_BLK].reshape(2, 1, 8, 8, AUX_BLK)
                for m in range(4)
            ]
            lanes.append(jnp.concatenate(parts, 1).reshape(512, AUX_BLK))
        moved = split(jnp.concatenate(lanes, 1))
        combined = dot3(left, moved).reshape(2, BAS, 8, 4 * AUX_BLK)
        lanes = []
        for f in range(2):
            parts = [
                combined[f, :, :, s_hi * AUX_BLK : (s_hi + 1) * AUX_BLK].reshape(BAS, 1, 8, AUX_BLK)
                for s_hi in range(4)
            ]
            lanes.append(jnp.concatenate(parts, 1).reshape(BAS * BAS, AUX_BLK))
        right = split(jnp.concatenate(lanes, 1))
        gath[0, me_r, p, pl.ds(0, 2 * AUX_BLK), :] = dot3(coef_all, right).astype(BF)
        y_copy(me_r, p).start()

        def send_row(dist, carry, p=p):
            @pl.when(me_r - dist >= 0)
            def _():
                z_copy(me_r, p, me_r - dist).start()

            @pl.when(me_r + dist < n_row)
            def _():
                z_copy(me_r, p, me_r + dist).start()

            return carry

        lax.fori_loop(1, n_row, send_row, 0)

    def assemble(side, s):
        labels = gath[side, s, 0, 2 * AUX_BLK :, 0:AUX_BLK].astype(F32)
        code = jnp.where(labels[8:16] == me_r.astype(F32), labels[0:8], -1.0)
        for p in range(2):
            for q in range(2):
                for f in range(2):
                    block = gath[
                        side, s, p, q * AUX_BLK : (q + 1) * AUX_BLK, f * AUX_BLK : (f + 1) * AUX_BLK
                    ].astype(F32)
                    prods[f, 2 * p + q] = block.T if side == 0 else block

        def tile_row(i, carry):
            rows = pl.ds(pl.multiple_of(i * AUX_BLK, AUX_BLK), AUX_BLK)
            for j in range(SUBS):
                sub = i * SUBS + j if side == 0 else j * SUBS + i
                counts = [
                    jnp.sum(
                        jnp.where(code == (sub * 4 + k).astype(F32), 1.0, 0.0), axis=0, keepdims=True
                    )
                    for k in range(4)
                ]
                for f in range(2):
                    cols = slice(j * AUX_BLK, (j + 1) * AUX_BLK)
                    total = out_ref[f, rows, cols]
                    for k in range(4):
                        total += counts[k] * prods[f, k]
                    out_ref[f, rows, cols] = total
            return carry

        lax.fori_loop(0, SUBS, tile_row, 0)

    assemble(0, me_r)

    def handed_copy():
        return pltpu.make_async_remote_copy(
            src_ref=item(1, me_r, 1),
            dst_ref=item(1, me_r, 1),
            send_sem=send_m.at[0],
            recv_sem=recv_y.at[me_r, 1],
            device_id=(buddy, me_c),
            device_id_type=MESH,
        )

    def pass_mirror(s, p):
        if p == 0:
            y_copy(s, p).start()
        else:

            @pl.when(s != buddy)
            def _():
                y_copy(s, p).start()

    def pass_on(dist, carry):
        low = me_r - dist
        high = me_r + dist
        for p in range(2):

            @pl.when(low >= 0)
            def _(p=p):
                z_copy(low, p, low).wait_recv()
                pass_mirror(low, p)

            @pl.when(high < n_row)
            def _(p=p):
                z_copy(high, p, high).wait_recv()
                pass_mirror(high, p)

        @pl.when(low >= 0)
        def _():
            assemble(0, low)

        @pl.when(high < n_row)
        def _():
            assemble(0, high)

        return carry

    lax.fori_loop(1, n_row, pass_on, 0)

    y_copy(me_r, 1).wait_recv()
    handed_copy().start()
    y_copy(me_r, 0).wait_recv()
    assemble(1, me_r)

    def take_mirror(s):
        for p in range(2):
            y_copy(s, p).wait_recv()
        assemble(1, s)

    def mirrored(dist, carry):
        low = me_r - dist
        high = me_r + dist

        @pl.when((low >= 0) & (low != buddy))
        def _():
            take_mirror(low)

        @pl.when((high < n_row) & (high != buddy))
        def _():
            take_mirror(high)

        return carry

    lax.fori_loop(1, n_row, mirrored, 0)
    take_mirror(buddy)
    handed_copy().wait_send()

    def drain_green(step, carry):
        green_copy(me_c, step, lax.rem(me_c + step, n_col)).wait_send()
        return carry

    lax.fori_loop(1, n_col, drain_green, 0)

    def drain(s, carry):
        for p in range(2):

            @pl.when((s != buddy) if p == 1 else (s >= 0))
            def _(p=p):
                y_copy(s, p).wait_send()

            @pl.when(s != me_r)
            def _(p=p):
                z_copy(me_r, p, s).wait_send()

        return carry

    lax.fori_loop(0, n_row, drain, 0)


def local(n_row, n_col, coefficients, greens, cosine_weights, block_atoms, pair_blocks, owner_row, target_sub):
    per = greens.shape[0]
    hbm = pl.BlockSpec(memory_space=pltpu.HBM)
    vmem = pl.BlockSpec(memory_space=pltpu.VMEM)
    tile = SUBS * AUX_BLK
    dma = pltpu.SemaphoreType.DMA
    return pl.pallas_call(
        functools.partial(kernel, n_row, n_col),
        out_shape=pltpu.VMEM((2, tile, tile), F32),
        in_specs=[hbm] * 7,
        out_specs=vmem,
        scratch_shapes=[
            pltpu.SMEM((2, 2), F32),
            pltpu.SMEM((2, 2), jnp.int32),
            pltpu.VMEM((2, 8), jnp.int32),
            pltpu.VMEM((1, 8), jnp.int32),
            pltpu.VMEM((1, 8), jnp.int32),
            pltpu.VMEM((2, AUX_BLK, BAS * BAS), F32),
            pltpu.VMEM((n_col, per, 4, BAS * BAS), F32),
            pltpu.VMEM((2, n_row, 2, 2 * AUX_BLK + LABEL_ROWS, 2 * AUX_BLK), BF),
            pltpu.VMEM((2, 4, AUX_BLK, AUX_BLK), F32),
            dma((7,)),
            dma((n_col,)),
            dma((n_col,)),
            dma((n_row, 2)),
            dma((n_row, 2)),
            dma((1,)),
            dma((n_row, 2)),
            dma((n_row, 2)),
        ],
        compiler_params=pltpu.CompilerParams(
            collective_id=0, has_side_effects=True, vmem_limit_bytes=60 * 1024 * 1024
        ),
    )(
        cosine_weights,
        block_atoms[0, 0],
        pair_blocks[0, 0].T,
        owner_row[0, 0].T,
        target_sub[0],
        greens,
        coefficients[0, 0],
    )


def solution(mesh):
    in_specs = (
        P("row", "col", None, None, None),
        P("col", None, None),
        P(),
        P("row", "col", None, None),
        P("row", "col", None, None),
        P("row", "col", None, None),
        P("row", "col", None),
    )
    return jax.shard_map(
        functools.partial(local, mesh.shape["row"], mesh.shape["col"]),
        mesh=mesh,
        in_specs=in_specs,
        out_specs=P(None, "row", "col"),
        check_vma=False,
    )
```

```python
import functools

import jax
import jax.numpy as jnp
from jax import lax
from jax.experimental import pallas as pl
from jax.experimental.pallas import tpu as pltpu
from jax.sharding import PartitionSpec as P

AUX_BLK = 128
BAS = 32
SUBS = 4
LABEL_ROWS = 16
BF = jnp.bfloat16
F32 = jnp.float32
MESH = pl.DeviceIdType.MESH


def split(x):
    high = x.astype(BF)
    return high, (x - high.astype(F32)).astype(BF)


def dot(a, b, dims=((1,), (0,))):
    return lax.dot_general(a, b, (dims, ((), ())), preferred_element_type=F32)


def dot3(a, b, dims=((1,), (0,))):
    return dot(a[0], b[0], dims) + (dot(a[0], b[1], dims) + dot(a[1], b[0], dims))


def onehot(shape, row_key, col_key):
    rows = lax.broadcasted_iota(jnp.int32, shape, 0)
    cols = lax.broadcasted_iota(jnp.int32, shape, 1)
    return row_key(rows) == col_key(cols)


def kernel(
    n_row, n_col, w_hbm, atoms_hbm, pairs_hbm, owners_hbm, targets_hbm, green_ref, coef_hbm, out_ref,
    w_ref, atoms_ref, pairs_ref, owners_ref, targets_ref, coef_ref,
    table, gath, prods, load, send_g, recv_g, send_l, send_r, send_y, send_m, recv_z, recv_y,
):
    me_r = lax.axis_index("row")
    me_c = lax.axis_index("col")
    half = n_col // 2
    mirror = lax.rem(me_c + half, n_col)
    per = green_ref.shape[0]
    buddy = me_r + 1 - 2 * lax.rem(me_r, 2)
    has_left = me_r > 0
    has_right = me_r < n_row - 1

    sources = (coef_hbm, green_ref, w_hbm, atoms_hbm, pairs_hbm, owners_hbm, targets_hbm)
    places = (coef_ref, table.at[me_c], w_ref, atoms_ref, pairs_ref, owners_ref, targets_ref)
    loads = [
        pltpu.make_async_copy(source, place, load.at[number])
        for number, (source, place) in enumerate(zip(sources, places))
    ]
    for copy in loads:
        copy.start()
    barrier = pltpu.get_barrier_semaphore()

    def greet(step, carry):
        peer = lax.rem(me_c + step, n_col)
        pl.semaphore_signal(barrier, inc=1, device_id=(me_r, peer), device_id_type=MESH)
        return carry

    lax.fori_loop(1, n_col, greet, 0)

    @pl.when(has_left)
    def _():
        pl.semaphore_signal(barrier, inc=1, device_id=(me_r - 1, me_c), device_id_type=MESH)

    @pl.when(has_right)
    def _():
        pl.semaphore_signal(barrier, inc=1, device_id=(me_r + 1, me_c), device_id_type=MESH)

    out_ref[...] = jnp.zeros_like(out_ref)
    pl.semaphore_wait(
        barrier, n_col - 1 + has_left.astype(jnp.int32) + has_right.astype(jnp.int32)
    )

    def green_copy(slot, step, peer):
        return pltpu.make_async_remote_copy(
            src_ref=green_ref,
            dst_ref=table.at[slot],
            send_sem=send_g.at[step],
            recv_sem=recv_g.at[slot],
            device_id=(me_r, peer),
            device_id_type=MESH,
        )

    def send_green(step, carry):
        green_copy(me_c, step, lax.rem(me_c + step, n_col)).start()
        return carry

    lax.fori_loop(1, n_col, send_green, 0)

    def item(side, s, p):
        rows = 2 * AUX_BLK + (LABEL_ROWS if p == 0 else 0)
        return gath.at[side, s, p, pl.ds(0, rows)]

    def z_copy(s, p, to_right):
        sems = send_r if to_right else send_l
        return pltpu.make_async_remote_copy(
            src_ref=item(0, s, p),
            dst_ref=item(0, s, p),
            send_sem=sems.at[s, p],
            recv_sem=recv_z.at[s, p],
            device_id=(me_r + 1 if to_right else me_r - 1, me_c),
            device_id_type=MESH,
        )

    def y_copy(s, p):
        return pltpu.make_async_remote_copy(
            src_ref=item(0, s, p),
            dst_ref=item(1, s, p),
            send_sem=send_y.at[s, p],
            recv_sem=recv_y.at[s, p],
            device_id=(me_r, mirror),
            device_id_type=MESH,
        )

    wide = 8 * BAS
    flat = BAS * BAS
    low_tile = onehot((flat, wide), lambda k: k // BAS, lambda j: j % BAS).astype(F32).astype(BF)
    low_each = onehot((flat, wide), lambda k: k // BAS, lambda j: j // 8).astype(F32).astype(BF)
    rep_each = onehot((wide, BAS), lambda i: i // 8, lambda k: k).astype(F32).astype(BF)
    row_pick = onehot((BAS, flat), lambda i: i, lambda k: k % BAS)
    mask_tile = onehot((wide, wide), lambda i: i // BAS, lambda j: j // BAS)
    mask_each = onehot((wide, wide), lambda i: i % 8, lambda j: j % 8)
    for copy in loads:
        copy.wait()
    diagonal = onehot((8, 8), lambda i: i, lambda j: j)
    pairs = pairs_ref[...]
    codes = targets_ref[...] * 4 + pairs[0:1] * 2 + pairs[1:2]
    labels = [
        jnp.broadcast_to(
            jnp.sum(jnp.where(diagonal, row.astype(F32), 0.0), axis=1, keepdims=True), (8, 2 * AUX_BLK)
        )
        for row in (codes, owners_ref[...])
    ]
    gath[0, me_r, 0, 2 * AUX_BLK :, :] = jnp.concatenate(labels, 0).astype(BF)
    coef = [split(coef_ref[q]) for q in range(2)]
    coef_all = tuple(jnp.concatenate([coef[q][h] for q in range(2)], 0) for h in range(2))

    def wait_green(step, carry):
        peer = lax.rem(me_c + step, n_col)
        green_copy(peer, step, peer).wait_recv()
        return carry

    lax.fori_loop(1, n_col, wait_green, 0)

    for p in range(2):
        first = atoms_ref[p, 0]
        second = atoms_ref[p, 1]
        own = table[first // per, first % per] if per > 1 else table[first, 0]
        other = table[second // per, second % per] if per > 1 else table[second, 0]
        occ = split(
            jnp.concatenate([jnp.where(row_pick, own[t : t + 1], 0.0) for t in range(2)], 0)
        )
        vir = split(
            jnp.concatenate([jnp.where(row_pick, other[2 + t : 3 + t], 0.0) for t in range(2)], 0)
        )
        virt = []
        for part in vir:
            spread = dot(part, low_tile)
            blocks = [
                jnp.where(mask_tile, jnp.concatenate([spread[t * BAS : (t + 1) * BAS]] * 8, 0), 0.0)
                for t in range(2)
            ]
            virt.append(jnp.concatenate(blocks, 0).astype(BF))
        spread = [dot(part, low_each).astype(BF) for part in occ]
        occupied = [
            jnp.where(
                mask_each, sum(dot(rep_each, part[t * BAS : (t + 1) * BAS]) for part in spread), 0.0
            )
            for t in range(2)
        ]
        left = split(
            jnp.concatenate(
                [
                    jnp.concatenate([occupied[t] * w_ref[f, t] for t in range(2)], 1)
                    for f in range(2)
                ],
                0,
            )
        )
        stacked = tuple(
            jnp.concatenate([part[:, m * wide : (m + 1) * wide] for m in range(4)], 0) for part in coef[p]
        )
        partway = dot3(virt, stacked, ((1,), (1,))).reshape(2, 8, 4, 8, 4 * AUX_BLK)
        lanes = []
        for s_hi in range(4):
            parts = [
                partway[:, :, s_hi, :, m * AUX_BLK : (m + 1) * AUX_BLK].reshape(2, 1, 8, 8, AUX_BLK)
                for m in range(4)
            ]
            lanes.append(jnp.concatenate(parts, 1).reshape(512, AUX_BLK))
        moved = split(jnp.concatenate(lanes, 1))
        combined = dot3(left, moved).reshape(2, BAS, 8, 4 * AUX_BLK)
        lanes = []
        for f in range(2):
            parts = [
                combined[f, :, :, s_hi * AUX_BLK : (s_hi + 1) * AUX_BLK].reshape(BAS, 1, 8, AUX_BLK)
                for s_hi in range(4)
            ]
            lanes.append(jnp.concatenate(parts, 1).reshape(BAS * BAS, AUX_BLK))
        right = split(jnp.concatenate(lanes, 1))
        gath[0, me_r, p, pl.ds(0, 2 * AUX_BLK), :] = dot3(coef_all, right).astype(BF)
        @pl.when(has_right)
        def _(p=p):
            z_copy(me_r, p, True).start()

        @pl.when(has_left)
        def _(p=p):
            z_copy(me_r, p, False).start()

        y_copy(me_r, p).start()

    def assemble(side, s):
        labels = gath[side, s, 0, 2 * AUX_BLK :, 0:AUX_BLK].astype(F32)
        code = jnp.where(labels[8:16] == me_r.astype(F32), labels[0:8], -1.0)
        for p in range(2):
            for q in range(2):
                for f in range(2):
                    block = gath[
                        side, s, p, q * AUX_BLK : (q + 1) * AUX_BLK, f * AUX_BLK : (f + 1) * AUX_BLK
                    ].astype(F32)
                    prods[f, 2 * p + q] = block.T if side == 0 else block

        def tile_row(i, carry):
            rows = pl.ds(pl.multiple_of(i * AUX_BLK, AUX_BLK), AUX_BLK)
            for j in range(SUBS):
                sub = i * SUBS + j if side == 0 else j * SUBS + i
                counts = [
                    jnp.sum(
                        jnp.where(code == (sub * 4 + k).astype(F32), 1.0, 0.0), axis=0, keepdims=True
                    )
                    for k in range(4)
                ]
                for f in range(2):
                    cols = slice(j * AUX_BLK, (j + 1) * AUX_BLK)
                    total = out_ref[f, rows, cols]
                    for k in range(4):
                        total += counts[k] * prods[f, k]
                    out_ref[f, rows, cols] = total
            return carry

        lax.fori_loop(0, SUBS, tile_row, 0)

    def handed_copy():
        return pltpu.make_async_remote_copy(
            src_ref=item(1, me_r, 1),
            dst_ref=item(1, me_r, 1),
            send_sem=send_m.at[0],
            recv_sem=recv_y.at[me_r, 1],
            device_id=(buddy, me_c),
            device_id_type=MESH,
        )

    def pass_mirror(s, p):
        if p == 0:
            y_copy(s, p).start()
        else:

            @pl.when(s != buddy)
            def _():
                y_copy(s, p).start()

    def pass_on(dist, carry):
        low = me_r - dist
        high = me_r + dist
        for p in range(2):

            @pl.when(low >= 0)
            def _(p=p):
                z_copy(low, p, True).wait_recv()

                @pl.when(has_right)
                def _():
                    z_copy(low, p, True).start()

                pass_mirror(low, p)

            @pl.when(high < n_row)
            def _(p=p):
                z_copy(high, p, False).wait_recv()

                @pl.when(has_left)
                def _():
                    z_copy(high, p, False).start()

                pass_mirror(high, p)

        return carry

    lax.fori_loop(1, n_row, pass_on, 0)

    y_copy(me_r, 1).wait_recv()
    handed_copy().start()

    def take_own(s, carry):
        assemble(0, s)
        return carry

    lax.fori_loop(0, n_row, take_own, 0)
    y_copy(me_r, 0).wait_recv()
    assemble(1, me_r)

    def take_mirror(s):
        for p in range(2):
            y_copy(s, p).wait_recv()
        assemble(1, s)

    def mirrored(dist, carry):
        low = me_r - dist
        high = me_r + dist

        @pl.when((low >= 0) & (low != buddy))
        def _():
            take_mirror(low)

        @pl.when((high < n_row) & (high != buddy))
        def _():
            take_mirror(high)

        return carry

    lax.fori_loop(1, n_row, mirrored, 0)
    take_mirror(buddy)
    handed_copy().wait_send()

    def drain_green(step, carry):
        green_copy(me_c, step, lax.rem(me_c + step, n_col)).wait_send()
        return carry

    lax.fori_loop(1, n_col, drain_green, 0)

    def drain(s, carry):
        for p in range(2):

            @pl.when((s != buddy) if p == 1 else (s >= 0))
            def _(p=p):
                y_copy(s, p).wait_send()

            @pl.when(has_right & (s <= me_r))
            def _(p=p):
                z_copy(s, p, True).wait_send()

            @pl.when(has_left & (s >= me_r))
            def _(p=p):
                z_copy(s, p, False).wait_send()

        return carry

    lax.fori_loop(0, n_row, drain, 0)


def local(n_row, n_col, coefficients, greens, cosine_weights, block_atoms, pair_blocks, owner_row, target_sub):
    per = greens.shape[0]
    hbm = pl.BlockSpec(memory_space=pltpu.HBM)
    vmem = pl.BlockSpec(memory_space=pltpu.VMEM)
    tile = SUBS * AUX_BLK
    dma = pltpu.SemaphoreType.DMA
    return pl.pallas_call(
        functools.partial(kernel, n_row, n_col),
        out_shape=pltpu.VMEM((2, tile, tile), F32),
        in_specs=[hbm] * 7,
        out_specs=vmem,
        scratch_shapes=[
            pltpu.SMEM((2, 2), F32),
            pltpu.SMEM((2, 2), jnp.int32),
            pltpu.VMEM((2, 8), jnp.int32),
            pltpu.VMEM((1, 8), jnp.int32),
            pltpu.VMEM((1, 8), jnp.int32),
            pltpu.VMEM((2, AUX_BLK, BAS * BAS), F32),
            pltpu.VMEM((n_col, per, 4, BAS * BAS), F32),
            pltpu.VMEM((2, n_row, 2, 2 * AUX_BLK + LABEL_ROWS, 2 * AUX_BLK), BF),
            pltpu.VMEM((2, 4, AUX_BLK, AUX_BLK), F32),
            dma((7,)),
            dma((n_col,)),
            dma((n_col,)),
            dma((n_row, 2)),
            dma((n_row, 2)),
            dma((n_row, 2)),
            dma((1,)),
            dma((n_row, 2)),
            dma((n_row, 2)),
        ],
        compiler_params=pltpu.CompilerParams(
            collective_id=0, has_side_effects=True, vmem_limit_bytes=60 * 1024 * 1024
        ),
    )(
        cosine_weights,
        block_atoms[0, 0],
        pair_blocks[0, 0].T,
        owner_row[0, 0].T,
        target_sub[0],
        greens,
        coefficients[0, 0],
    )


def solution(mesh):
    in_specs = (
        P("row", "col", None, None, None),
        P("col", None, None),
        P(),
        P("row", "col", None, None),
        P("row", "col", None, None),
        P("row", "col", None, None),
        P("row", "col", None),
    )
    return jax.shard_map(
        functools.partial(local, mesh.shape["row"], mesh.shape["col"]),
        mesh=mesh,
        in_specs=in_specs,
        out_specs=P(None, "row", "col"),
        check_vma=False,
    )
```

```python
import functools

import jax
import jax.numpy as jnp
from jax import lax
from jax.experimental import pallas as pl
from jax.experimental.pallas import tpu as pltpu
from jax.sharding import PartitionSpec as P

AUX_BLK = 128
BAS = 32
SUBS = 4
LABEL_ROWS = 16
BF = jnp.bfloat16
F32 = jnp.float32
MESH = pl.DeviceIdType.MESH


def split(x):
    high = x.astype(BF)
    return high, (x - high.astype(F32)).astype(BF)


def dot(a, b, dims=((1,), (0,))):
    return lax.dot_general(a, b, (dims, ((), ())), preferred_element_type=F32)


def dot3(a, b, dims=((1,), (0,))):
    return dot(a[0], b[0], dims) + (dot(a[0], b[1], dims) + dot(a[1], b[0], dims))


def onehot(shape, row_key, col_key):
    rows = lax.broadcasted_iota(jnp.int32, shape, 0)
    cols = lax.broadcasted_iota(jnp.int32, shape, 1)
    return row_key(rows) == col_key(cols)


def kernel(
    n_row, n_col, w_hbm, atoms_hbm, pairs_hbm, owners_hbm, targets_hbm, green_ref, coef_hbm, out_ref,
    w_ref, atoms_ref, pairs_ref, owners_ref, targets_ref, coef_ref,
    table, gath, prods, load, send_g, recv_g, send_l, send_r, send_y, send_m, recv_z, recv_y,
):
    me_r = lax.axis_index("row")
    me_c = lax.axis_index("col")
    half = n_col // 2
    mirror = lax.rem(me_c + half, n_col)
    per = green_ref.shape[0]
    buddy = me_r + 1 - 2 * lax.rem(me_r, 2)
    has_left = me_r > 0
    has_right = me_r < n_row - 1

    sources = (coef_hbm, green_ref, w_hbm, atoms_hbm, pairs_hbm, owners_hbm, targets_hbm)
    places = (coef_ref, table.at[me_c], w_ref, atoms_ref, pairs_ref, owners_ref, targets_ref)
    loads = [
        pltpu.make_async_copy(source, place, load.at[number])
        for number, (source, place) in enumerate(zip(sources, places))
    ]
    for copy in loads:
        copy.start()
    barrier = pltpu.get_barrier_semaphore()

    def greet(step, carry):
        peer = lax.rem(me_c + step, n_col)
        pl.semaphore_signal(barrier, inc=1, device_id=(me_r, peer), device_id_type=MESH)
        return carry

    lax.fori_loop(1, n_col, greet, 0)

    @pl.when(has_left)
    def _():
        pl.semaphore_signal(barrier, inc=1, device_id=(me_r - 1, me_c), device_id_type=MESH)

    @pl.when(has_right)
    def _():
        pl.semaphore_signal(barrier, inc=1, device_id=(me_r + 1, me_c), device_id_type=MESH)

    out_ref[...] = jnp.zeros_like(out_ref)
    pl.semaphore_wait(
        barrier, n_col - 1 + has_left.astype(jnp.int32) + has_right.astype(jnp.int32)
    )

    def green_copy(slot, step, peer):
        return pltpu.make_async_remote_copy(
            src_ref=green_ref,
            dst_ref=table.at[slot],
            send_sem=send_g.at[step],
            recv_sem=recv_g.at[slot],
            device_id=(me_r, peer),
            device_id_type=MESH,
        )

    def send_green(step, carry):
        green_copy(me_c, step, lax.rem(me_c + step, n_col)).start()
        return carry

    lax.fori_loop(1, n_col, send_green, 0)

    def item(side, s, p):
        rows = 2 * AUX_BLK + (LABEL_ROWS if p == 0 else 0)
        return gath.at[side, s, p, pl.ds(0, rows)]

    def z_copy(s, p, to_right):
        sems = send_r if to_right else send_l
        return pltpu.make_async_remote_copy(
            src_ref=item(0, s, p),
            dst_ref=item(0, s, p),
            send_sem=sems.at[s, p],
            recv_sem=recv_z.at[s, p],
            device_id=(me_r + 1 if to_right else me_r - 1, me_c),
            device_id_type=MESH,
        )

    def y_copy(s, p):
        return pltpu.make_async_remote_copy(
            src_ref=item(0, s, p),
            dst_ref=item(1, s, p),
            send_sem=send_y.at[s, p],
            recv_sem=recv_y.at[s, p],
            device_id=(me_r, mirror),
            device_id_type=MESH,
        )

    wide = 8 * BAS
    flat = BAS * BAS
    low_tile = onehot((flat, wide), lambda k: k // BAS, lambda j: j % BAS).astype(F32).astype(BF)
    low_each = onehot((flat, wide), lambda k: k // BAS, lambda j: j // 8).astype(F32).astype(BF)
    rep_each = onehot((wide, BAS), lambda i: i // 8, lambda k: k).astype(F32).astype(BF)
    row_pick = onehot((BAS, flat), lambda i: i, lambda k: k % BAS)
    mask_tile = onehot((wide, wide), lambda i: i // BAS, lambda j: j // BAS)
    mask_each = onehot((wide, wide), lambda i: i % 8, lambda j: j % 8)
    for copy in loads:
        copy.wait()
    diagonal = onehot((8, 8), lambda i: i, lambda j: j)
    pairs = pairs_ref[...]
    codes = targets_ref[...] * 4 + pairs[0:1] * 2 + pairs[1:2]
    labels = [
        jnp.broadcast_to(
            jnp.sum(jnp.where(diagonal, row.astype(F32), 0.0), axis=1, keepdims=True), (8, 2 * AUX_BLK)
        )
        for row in (codes, owners_ref[...])
    ]
    gath[0, me_r, 0, 2 * AUX_BLK :, :] = jnp.concatenate(labels, 0).astype(BF)
    coef = [split(coef_ref[q]) for q in range(2)]
    coef_all = tuple(jnp.concatenate([coef[q][h] for q in range(2)], 0) for h in range(2))

    def wait_green(step, carry):
        peer = lax.rem(me_c + step, n_col)
        green_copy(peer, step, peer).wait_recv()
        return carry

    lax.fori_loop(1, n_col, wait_green, 0)

    for p in range(2):
        first = atoms_ref[p, 0]
        second = atoms_ref[p, 1]
        own = table[first // per, first % per] if per > 1 else table[first, 0]
        other = table[second // per, second % per] if per > 1 else table[second, 0]
        occ = split(
            jnp.concatenate([jnp.where(row_pick, own[t : t + 1], 0.0) for t in range(2)], 0)
        )
        vir = split(
            jnp.concatenate([jnp.where(row_pick, other[2 + t : 3 + t], 0.0) for t in range(2)], 0)
        )
        virt = []
        for part in vir:
            spread = dot(part, low_tile)
            blocks = [
                jnp.where(mask_tile, jnp.concatenate([spread[t * BAS : (t + 1) * BAS]] * 8, 0), 0.0)
                for t in range(2)
            ]
            virt.append(jnp.concatenate(blocks, 0).astype(BF))
        spread = [dot(part, low_each).astype(BF) for part in occ]
        occupied = [
            jnp.where(
                mask_each, sum(dot(rep_each, part[t * BAS : (t + 1) * BAS]) for part in spread), 0.0
            )
            for t in range(2)
        ]
        left = split(
            jnp.concatenate(
                [
                    jnp.concatenate([occupied[t] * w_ref[f, t] for t in range(2)], 1)
                    for f in range(2)
                ],
                0,
            )
        )
        stacked = tuple(
            jnp.concatenate([part[:, m * wide : (m + 1) * wide] for m in range(4)], 0) for part in coef[p]
        )
        partway = dot3(virt, stacked, ((1,), (1,))).reshape(2, 8, 4, 8, 4 * AUX_BLK)
        lanes = []
        for s_hi in range(4):
            parts = [
                partway[:, :, s_hi, :, m * AUX_BLK : (m + 1) * AUX_BLK].reshape(2, 1, 8, 8, AUX_BLK)
                for m in range(4)
            ]
            lanes.append(jnp.concatenate(parts, 1).reshape(512, AUX_BLK))
        moved = split(jnp.concatenate(lanes, 1))
        combined = dot3(left, moved).reshape(2, BAS, 8, 4 * AUX_BLK)
        lanes = []
        for f in range(2):
            parts = [
                combined[f, :, :, s_hi * AUX_BLK : (s_hi + 1) * AUX_BLK].reshape(BAS, 1, 8, AUX_BLK)
                for s_hi in range(4)
            ]
            lanes.append(jnp.concatenate(parts, 1).reshape(BAS * BAS, AUX_BLK))
        right = split(jnp.concatenate(lanes, 1))
        gath[0, me_r, p, pl.ds(0, 2 * AUX_BLK), :] = dot3(coef_all, right).astype(BF)
        @pl.when(has_right)
        def _(p=p):
            z_copy(me_r, p, True).start()

        @pl.when(has_left)
        def _(p=p):
            z_copy(me_r, p, False).start()

        y_copy(me_r, p).start()

    def assemble(side, s):
        labels = gath[side, s, 0, 2 * AUX_BLK :, 0:AUX_BLK].astype(F32)
        code = jnp.where(labels[8:16] == me_r.astype(F32), labels[0:8], -1.0)
        for p in range(2):
            for q in range(2):
                for f in range(2):
                    block = gath[
                        side, s, p, q * AUX_BLK : (q + 1) * AUX_BLK, f * AUX_BLK : (f + 1) * AUX_BLK
                    ].astype(F32)
                    prods[f, 2 * p + q] = block.T if side == 0 else block

        def tile_row(i, carry):
            rows = pl.ds(pl.multiple_of(i * AUX_BLK, AUX_BLK), AUX_BLK)
            for j in range(SUBS):
                sub = i * SUBS + j if side == 0 else j * SUBS + i
                counts = [
                    jnp.sum(
                        jnp.where(code == (sub * 4 + k).astype(F32), 1.0, 0.0), axis=0, keepdims=True
                    )
                    for k in range(4)
                ]
                for f in range(2):
                    cols = slice(j * AUX_BLK, (j + 1) * AUX_BLK)
                    total = out_ref[f, rows, cols]
                    for k in range(4):
                        total += counts[k] * prods[f, k]
                    out_ref[f, rows, cols] = total
            return carry

        lax.fori_loop(0, SUBS, tile_row, 0)

    assemble(0, me_r)

    def handed_copy():
        return pltpu.make_async_remote_copy(
            src_ref=item(1, me_r, 1),
            dst_ref=item(1, me_r, 1),
            send_sem=send_m.at[0],
            recv_sem=recv_y.at[me_r, 1],
            device_id=(buddy, me_c),
            device_id_type=MESH,
        )

    def pass_mirror(s, p):
        if p == 0:
            y_copy(s, p).start()
        else:

            @pl.when(s != buddy)
            def _():
                y_copy(s, p).start()

    def pass_on(dist, carry):
        low = me_r - dist
        high = me_r + dist
        for p in range(2):

            @pl.when(low >= 0)
            def _(p=p):
                z_copy(low, p, True).wait_recv()
                pass_mirror(low, p)

                @pl.when(has_right)
                def _():
                    z_copy(low, p, True).start()

            @pl.when(high < n_row)
            def _(p=p):
                z_copy(high, p, False).wait_recv()
                pass_mirror(high, p)

                @pl.when(has_left)
                def _():
                    z_copy(high, p, False).start()

        @pl.when(low >= 0)
        def _():
            assemble(0, low)

        @pl.when(high < n_row)
        def _():
            assemble(0, high)

        return carry

    lax.fori_loop(1, n_row, pass_on, 0)

    y_copy(me_r, 1).wait_recv()
    handed_copy().start()
    y_copy(me_r, 0).wait_recv()
    assemble(1, me_r)

    def take_mirror(s):
        for p in range(2):
            y_copy(s, p).wait_recv()
        assemble(1, s)

    def mirrored(dist, carry):
        low = me_r - dist
        high = me_r + dist

        @pl.when((low >= 0) & (low != buddy))
        def _():
            take_mirror(low)

        @pl.when((high < n_row) & (high != buddy))
        def _():
            take_mirror(high)

        return carry

    lax.fori_loop(1, n_row, mirrored, 0)
    take_mirror(buddy)
    handed_copy().wait_send()

    def drain_green(step, carry):
        green_copy(me_c, step, lax.rem(me_c + step, n_col)).wait_send()
        return carry

    lax.fori_loop(1, n_col, drain_green, 0)

    def drain(s, carry):
        for p in range(2):

            @pl.when((s != buddy) if p == 1 else (s >= 0))
            def _(p=p):
                y_copy(s, p).wait_send()

            @pl.when(has_right & (s <= me_r))
            def _(p=p):
                z_copy(s, p, True).wait_send()

            @pl.when(has_left & (s >= me_r))
            def _(p=p):
                z_copy(s, p, False).wait_send()

        return carry

    lax.fori_loop(0, n_row, drain, 0)


def local(n_row, n_col, coefficients, greens, cosine_weights, block_atoms, pair_blocks, owner_row, target_sub):
    per = greens.shape[0]
    hbm = pl.BlockSpec(memory_space=pltpu.HBM)
    vmem = pl.BlockSpec(memory_space=pltpu.VMEM)
    tile = SUBS * AUX_BLK
    dma = pltpu.SemaphoreType.DMA
    return pl.pallas_call(
        functools.partial(kernel, n_row, n_col),
        out_shape=pltpu.VMEM((2, tile, tile), F32),
        in_specs=[hbm] * 7,
        out_specs=vmem,
        scratch_shapes=[
            pltpu.SMEM((2, 2), F32),
            pltpu.SMEM((2, 2), jnp.int32),
            pltpu.VMEM((2, 8), jnp.int32),
            pltpu.VMEM((1, 8), jnp.int32),
            pltpu.VMEM((1, 8), jnp.int32),
            pltpu.VMEM((2, AUX_BLK, BAS * BAS), F32),
            pltpu.VMEM((n_col, per, 4, BAS * BAS), F32),
            pltpu.VMEM((2, n_row, 2, 2 * AUX_BLK + LABEL_ROWS, 2 * AUX_BLK), BF),
            pltpu.VMEM((2, 4, AUX_BLK, AUX_BLK), F32),
            dma((7,)),
            dma((n_col,)),
            dma((n_col,)),
            dma((n_row, 2)),
            dma((n_row, 2)),
            dma((n_row, 2)),
            dma((1,)),
            dma((n_row, 2)),
            dma((n_row, 2)),
        ],
        compiler_params=pltpu.CompilerParams(
            collective_id=0, has_side_effects=True, vmem_limit_bytes=60 * 1024 * 1024
        ),
    )(
        cosine_weights,
        block_atoms[0, 0],
        pair_blocks[0, 0].T,
        owner_row[0, 0].T,
        target_sub[0],
        greens,
        coefficients[0, 0],
    )


def solution(mesh):
    in_specs = (
        P("row", "col", None, None, None),
        P("col", None, None),
        P(),
        P("row", "col", None, None),
        P("row", "col", None, None),
        P("row", "col", None, None),
        P("row", "col", None),
    )
    return jax.shard_map(
        functools.partial(local, mesh.shape["row"], mesh.shape["col"]),
        mesh=mesh,
        in_specs=in_specs,
        out_specs=P(None, "row", "col"),
        check_vma=False,
    )
```
